32 devices in a mesh: rep: 8 (over y, x, core), shard: 4 (over z).
Axes of the slice: x: 2, y: 2, z: 4, core: 2. Of those that a mesh axis runs over, the one named last changes fastest.
Arguments:
- grad_embed: bfloat16 [8, 4, 2048, 768], P('rep', 'shard'), may hold values from -800 to 800
- grad_proj: bfloat16 [8, 4, 768, 768], P('rep', 'shard'), may hold values from -800 to 800
- grad_norms: bfloat16 [8, 4, 4, 768], P('rep', 'shard'), may hold values from -800 to 800
- embed_master: float32 [2048, 768], P('shard'), may hold values from -0.75 to 0.75
- embed_first: float32 [2048, 768], P('shard'), may hold values from -6 to 6
- embed_second: float32 [2048, 768], P('shard'), may hold values from 0.01 to 4
- proj_master: float32 [768, 768], P('shard'), may hold values from -0.21875 to 0.21875
- proj_first: float32 [768, 768], P('shard'), may hold values from -6 to 6
- proj_second: float32 [768, 768], P('shard'), may hold values from 0.01 to 4
- norm_master: float32 [4, 768], P(None, 'shard'), may hold values from -6 to 6
- norm_first: float32 [4, 768], P(None, 'shard'), may hold values from -6 to 6
- norm_second: float32 [4, 768], P(None, 'shard'), may hold values from 0.01 to 4
Outputs:
- embed_master_new: float32 [2048, 768], P('shard')
- embed_first_new: float32 [2048, 768], P('shard')
- embed_second_new: float32 [2048, 768], P('shard')
- embed_weights: bfloat16 [2048, 768], replicated
- proj_master_new: float32 [768, 768], P('shard')
- proj_first_new: float32 [768, 768], P('shard')
- proj_second_new: float32 [768, 768], P('shard')
- proj_weights: bfloat16 [768, 768], replicated
- norm_master_new: float32 [4, 768], P(None, 'shard')
- norm_first_new: float32 [4, 768], P(None, 'shard')
- norm_second_new: float32 [4, 768], P(None, 'shard')
- norm_weights: bfloat16 [4, 768], replicated
The draws below stay inside these ranges and needn't reach their ends.
All inputs are finite; a program needn't handle non-finite values.
Results may differ from the reference program's by a relative error of at most 0.0004.
Values may be sent and summed in bfloat16 or wider, within the bound.
A program may use at most 128 MiB of HBM per device.

```python
import math
import jax
import jax.numpy as jnp
from jax import lax

D = 768
EMB = 2048
N_REP = 8
N_SHARD = 4


def rough_grad(key, row_count, col_count, band_rows):
    first_key = jax.random.fold_in(key, 0)
    second_key = jax.random.fold_in(key, 1)
    fourth_key = jax.random.fold_in(key, 3)
    full_shape = (N_REP, N_SHARD, row_count, col_count)
    row_scale = 10.0 ** jax.random.uniform(second_key, (row_count, 1), jnp.float32)
    col_scale = 10.0 ** jax.random.uniform(fourth_key, (1, col_count), jnp.float32)
    shard_index = jnp.arange(N_SHARD, dtype=jnp.int32)[None, :, None, None]
    if band_rows:
        band_index = (jnp.arange(row_count, dtype=jnp.int32) // (row_count // N_SHARD))[None, None, :, None]
    else:
        band_index = (jnp.arange(col_count, dtype=jnp.int32) // (col_count // N_SHARD))[None, None, None, :]
    band_boost = jnp.where(band_index == shard_index, 3.0, 1.0).astype(jnp.float32)
    band_level = band_index.astype(jnp.float32) / float(max(N_SHARD - 1, 1))
    band_rise = (1.0 + 2.0 * band_level) / 3.0
    base_values = 0.5 * jnp.clip(jax.random.normal(first_key, full_shape, jnp.float32), -5.0, 5.0)
    return (base_values * band_rise * band_boost * row_scale * col_scale).astype(jnp.bfloat16)


def draw_grad_embed(key, part):
    return rough_grad(jax.random.fold_in(key, 11), EMB, D, True)


def draw_grad_proj(key, part):
    return rough_grad(jax.random.fold_in(key, 12), D, D, True)


def draw_grad_norms(key, part):
    return rough_grad(jax.random.fold_in(key, 13), 4, D, False)


def levels(stream_key, shape, shards, low, high):
    def one(dim, shards_of):
        steps = jax.random.uniform(jax.random.fold_in(jax.random.fold_in(stream_key, 6), dim), (shards_of,), jnp.float32, low / len(shards), high / len(shards))
        return jnp.repeat(jnp.exp(steps), shape[dim] // shards_of).reshape((-1,) + (1,) * (len(shape) - dim - 1))

    gain = one(*shards[0])
    for cut in shards[1:]:
        gain = gain * one(*cut)
    return gain


def scatter_about(stream_key, extent, spread, reach, shards=(), held_as=jnp.bfloat16):
    drawn = jax.random.normal(stream_key, extent, jnp.float32) * spread
    if len(shards) > 0:
        drawn = levels(stream_key, extent, shards, -0.22, 0.18) * drawn
    return jnp.clip(drawn, min=-reach, max=reach).astype(held_as)


def setup_inputs(seed: int = 0) -> dict:
    key_of = jax.random.split(jax.random.key(seed), 13)
    return {
        "grad_embed": draw_grad_embed(jax.random.fold_in(key_of[12], 71), 0),
        "grad_proj": draw_grad_proj(jax.random.fold_in(key_of[12], 71), 0),
        "grad_norms": draw_grad_norms(jax.random.fold_in(key_of[12], 71), 0),
        "embed_master": scatter_about(key_of[3], (EMB, D), 0.05, 0.75, ((0, 4),), jnp.float32),
        "embed_first": scatter_about(key_of[4], (EMB, D), 0.5, 6.0, ((0, 4),), jnp.float32),
        "embed_second": jnp.clip(jnp.exp(math.log(4.0) - 5.9914646 * jax.random.uniform(key_of[5], (EMB, D), jnp.float32) ** levels(key_of[5], (EMB, D), ((0, 4),), -0.2, 0.2)), 0.01, 4.0),
        "proj_master": scatter_about(key_of[6], (D, D), D ** -0.5, 0.21875, ((0, 4),), jnp.float32),
        "proj_first": scatter_about(key_of[7], (D, D), 0.5, 6.0, ((0, 4),), jnp.float32),
        "proj_second": jnp.clip(jnp.exp(math.log(4.0) - 5.9914646 * jax.random.uniform(key_of[8], (D, D), jnp.float32) ** levels(key_of[8], (D, D), ((0, 4),), -0.2, 0.2)), 0.01, 4.0),
        "norm_master": scatter_about(key_of[9], (4, D), 0.5, 6.0, ((1, 4),), jnp.float32),
        "norm_first": scatter_about(key_of[10], (4, D), 0.5, 6.0, ((1, 4),), jnp.float32),
        "norm_second": jnp.clip(jnp.exp(math.log(4.0) - 5.9914646 * jax.random.uniform(key_of[11], (4, D), jnp.float32) ** levels(key_of[11], (4, D), ((1, 4),), -0.2, 0.2)), 0.01, 4.0),
    }


beta_one = 0.9
beta_two = 0.95
adam_step = 10.0
adam_eps = 1e-08
learning_rate = 0.002
clip_rms = 1.0

def accumulate(grads):
    flat = grads.reshape((-1,) + grads.shape[2:])

    def add_term(running, device_term):
        return (running + device_term.astype(jnp.float32), None)
    running, _ = lax.scan(add_term, jnp.zeros(grads.shape[2:], jnp.float32), flat)
    return running

def adamw(gradient, master, first, second, weight_decay):
    corr_one = 1.0 - beta_one ** adam_step
    corr_two = 1.0 - beta_two ** adam_step
    first_new = beta_one * first + (1.0 - beta_one) * gradient
    second_new = beta_two * second + (1.0 - beta_two) * gradient * gradient
    direction = first_new / corr_one / (jnp.sqrt(second_new / corr_two) + adam_eps) + weight_decay * master
    master_new = master - learning_rate * direction
    return (master_new, first_new, second_new, master_new.astype(jnp.bfloat16))

def reference(grad_embed, grad_proj, grad_norms, embed_master, embed_first, embed_second, proj_master, proj_first, proj_second, norm_master, norm_first, norm_second):
    embed_sum = accumulate(grad_embed)
    proj_sum = accumulate(grad_proj)
    norm_sum = accumulate(grad_norms)
    squares = jnp.sum(embed_sum * embed_sum) + jnp.sum(proj_sum * proj_sum) + jnp.sum(norm_sum * norm_sum)
    entry_count = float(EMB * D + D * D + 4 * D)
    rms_value = jnp.sqrt(squares / entry_count)
    clip_factor = jnp.minimum(jnp.float32(1.0), clip_rms / (rms_value + 1e-06))
    embed_out = adamw(clip_factor * embed_sum, embed_master, embed_first, embed_second, 0.01)
    proj_out = adamw(clip_factor * proj_sum, proj_master, proj_first, proj_second, 0.01)
    norm_out = adamw(clip_factor * norm_sum, norm_master, norm_first, norm_second, 0.0)
    return (embed_out[0], embed_out[1], embed_out[2], embed_out[3], proj_out[0], proj_out[1], proj_out[2], proj_out[3], norm_out[0], norm_out[1], norm_out[2], norm_out[3])
```

```python
import functools

import jax
import jax.numpy as jnp
from jax import lax
from jax.experimental import pallas as pl
from jax.experimental.pallas import tpu as pltpu
from jax.sharding import PartitionSpec as P

beta_one = 0.9
beta_two = 0.95
adam_step = 10.0
adam_eps = 1e-08
learning_rate = 0.002
clip_rms = 1.0
LANES = 128
MESH = pl.DeviceIdType.MESH


def adamw(gradient, master, first, second, weight_decay):
    corr_one = 1.0 - beta_one**adam_step
    corr_two = 1.0 - beta_two**adam_step
    first_new = beta_one * first + (1.0 - beta_one) * gradient
    second_new = beta_two * second + (1.0 - beta_two) * gradient * gradient
    direction = (
        first_new / corr_one / (jnp.sqrt(second_new / corr_two) + adam_eps) + weight_decay * master
    )
    master_new = master - learning_rate * direction
    return (master_new, first_new, second_new)


def bit_of(index, bit):
    return lax.rem(lax.div(index, 1 << bit), 2)


def flipped(index, mask):
    bit = 0
    out = index
    while mask >> bit:
        if (mask >> bit) & 1:
            out = out + (1 - 2 * bit_of(index, bit)) * (1 << bit)
        bit += 1
    return out


def tile_sum(values):
    return jnp.sum(values.reshape(values.shape[0] // 8, 8, LANES), axis=0)


def kernel(
    plan,
    grad_embed, grad_proj, grad_norm,
    embed_m, embed_f, embed_s, proj_m, proj_f, proj_s, norm_m, norm_f, norm_s,
    out_em, out_ef, out_es, out_ew, out_pm, out_pf, out_ps, out_pw,
    out_nm, out_nf, out_ns, out_nw,
    own_e, own_p, got_e, got_p, work, sums,
    state_em, state_ef, state_es, state_pm, state_pf, state_ps, local_ew, local_pw,
    norm_acc, norm_got, norm_w, square_acc, square_got, factor_ref,
    *rest,
):
    reps, shards, chunks, e_half, p_half, half_rows, entry_count = plan
    send_sem, recv_sem, local_sem = rest[-3:]
    landed = rest[:-3]
    rep_bits = reps.bit_length() - 1
    shard_bits = shards.bit_length() - 1
    subs = reps // 2
    block = half_rows // subs
    piece = e_half // subs
    rep = lax.axis_index("rep")
    shard = lax.axis_index("shard")
    core = lax.rem(rep, 2)
    sub = lax.div(rep, 2)
    where = {"rep": rep, "shard": shard}
    all_bits = [("rep", b) for b in range(rep_bits)] + [("shard", b) for b in range(shard_bits)]

    sends = []
    locals_ = []

    def send(src, dst, axis, bit):
        i = len(sends)
        copy = pltpu.make_async_remote_copy(
            src_ref=src, dst_ref=dst, send_sem=send_sem.at[i], recv_sem=recv_sem.at[i],
            device_id={axis: flipped(where[axis], 1 << bit)}, device_id_type=MESH,
        )
        copy.start()
        sends.append(copy)
        return copy

    def local(src, dst):
        copy = pltpu.make_async_copy(src, dst, local_sem.at[len(locals_)])
        copy.start()
        locals_.append(copy)
        return copy

    ascending = list(range(1, rep_bits))
    half_chunks = max(chunks // 2, 1)

    def rep_order(c):
        return ascending if c < half_chunks else ascending[::-1]

    turn = []
    for i in range(half_chunks):
        turn += [c for c in (i, i + half_chunks) if c < chunks]

    own = {}
    for c in turn:
        cols = pl.ds(c * LANES, LANES)
        own[c] = (
            local(grad_embed.at[:, core, :, cols], own_e.at[c]),
            local(grad_proj.at[:, core, :, cols], own_p.at[c]),
        )
    barrier = pltpu.get_barrier_semaphore()
    for axis, b in all_bits:
        pl.semaphore_signal(
            barrier, inc=1, device_id={axis: flipped(where[axis], 1 << b)}, device_id_type=MESH
        )
    pl.semaphore_wait(barrier, len(all_bits))

    other = 1 - core
    first_hop = {}
    for c in turn:
        cols = pl.ds(c * LANES, LANES)
        first_hop[c] = (
            send(grad_embed.at[:, other, :, cols], got_e.at[c], "rep", 0),
            send(grad_proj.at[:, other, :, cols], got_p.at[c], "rep", 0),
        )
    states = [
        local(src, dst)
        for src, dst in (
            (embed_m, state_em), (embed_f, state_ef), (embed_s, state_es),
            (proj_m, state_pm), (proj_f, state_pf), (proj_s, state_ps),
        )
    ]

    norm_acc[0] = grad_norm[...].astype(jnp.float32)
    norm_copy = send(norm_acc.at[0], norm_got.at[0], *all_bits[0])
    norm_round = 0

    dims = [("shard", b) for b in reversed(range(shard_bits))]
    dims += [("rep", b) for b in reversed(range(1, rep_bits))]

    def region(c, done, dim=None, value=None):
        index = [c]
        for d in dims:
            if d == dim:
                index.append(value)
            elif d in done:
                index.append(bit_of(where[d[0]], d[1]))
            else:
                index.append(slice(None))
        return tuple(index)

    def stage_order(c):
        return [("rep", b) for b in rep_order(c)] + [("shard", b) for b in range(shard_bits)]

    hops = {}

    def start_hop(c, k):
        order = stage_order(c)
        dim = order[k]
        theirs = 1 - bit_of(where[dim[0]], dim[1])
        hops[c] = send(work.at[region(c, order[:k], dim, theirs)], landed[k].at[c], *dim)

    for c in turn:
        for copy in own[c]:
            copy.wait()
        for copy in first_hop[c]:
            copy.wait_recv()
        for s in range(shards):
            parts = [
                own_e[c, s].astype(jnp.float32) + got_e[c, s].astype(jnp.float32),
                own_p[c, s].astype(jnp.float32) + got_p[c, s].astype(jnp.float32),
            ]
            pad = half_rows - e_half - p_half
            if pad:
                parts.append(jnp.zeros((pad, LANES), jnp.float32))
            slab = jnp.concatenate(parts, axis=0)
            index = (c,) + tuple((s >> b) & 1 for b in reversed(range(shard_bits)))
            work[index] = slab.reshape((2,) * (rep_bits - 1) + (block, LANES))
        start_hop(c, 0)

    gathers = {}
    masks_of = {c: [0] for c in turn}

    def sub_rows(mask):
        return pl.ds(pl.multiple_of(flipped(sub, mask) * block, 8), block)

    def start_gather(c, t):
        order = rep_order(c)[::-1]
        gathers[c] = []
        if t < len(order):
            for mask in masks_of[c]:
                ref = sums.at[c, core, sub_rows(mask)]
                gathers[c].append(send(ref, ref, "rep", order[t]))
            masks_of[c] = masks_of[c] + [m | 1 << (order[t] - 1) for m in masks_of[c]]
        else:
            ref = sums.at[c, core]
            gathers[c].append(send(ref, ref, "rep", 0))

    def advance_norm(current):
        copy, done = current
        if copy is None:
            return current
        copy.wait_recv()
        norm_acc[done + 1] = norm_acc[done] + norm_got[done]
        done += 1
        if done < len(all_bits):
            return send(norm_acc.at[done], norm_got.at[done], *all_bits[done]), done
        return None, done

    current = (norm_copy, 0)
    squares = jnp.zeros((8, LANES), jnp.float32)
    for k in range(len(dims)):
        for c in turn:
            order = stage_order(c)
            dim = order[k]
            hops[c].wait_recv()
            index = region(c, order[:k], dim, bit_of(where[dim[0]], dim[1]))
            total = work[index] + landed[k][c]
            if k + 1 < len(dims):
                work[index] = total
                start_hop(c, k + 1)
            else:
                sums[c, core, sub_rows(0), :] = total
                squares = squares + tile_sum(total * total)
                start_gather(c, 0)
        current = advance_norm(current)
    while current[0] is not None:
        current = advance_norm(current)

    square_acc[0] = squares
    square_copy = send(square_acc.at[0], square_got.at[0], *all_bits[0])
    rounds = 0

    def advance_square(copy, done):
        copy.wait_recv()
        square_acc[done + 1] = square_acc[done] + square_got[done]
        done += 1
        if done < len(all_bits):
            return send(square_acc.at[done], square_got.at[done], *all_bits[done]), done
        return None, done

    for t in range(1, rep_bits):
        for c in turn:
            for copy in gathers[c]:
                copy.wait_recv()
            start_gather(c, t)
        if square_copy is not None:
            square_copy, rounds = advance_square(square_copy, rounds)
    while square_copy is not None:
        square_copy, rounds = advance_square(square_copy, rounds)
    for c in turn:
        for copy in gathers[c]:
            copy.wait_recv()

    norm_sum = norm_acc[len(all_bits)]
    total = jnp.sum(square_acc[len(all_bits)], axis=(0, 1), keepdims=True)
    total = total + jnp.sum(norm_sum * norm_sum, axis=(0, 1), keepdims=True)
    rms = jnp.sqrt(total / entry_count)
    factor = jnp.minimum(jnp.float32(1.0), clip_rms / (rms + 1e-06))
    factor_ref[...] = jnp.broadcast_to(factor, factor_ref.shape)
    for copy in states:
        copy.wait()

    def update(refs, weights, half, base, core_index):
        rows = 32 if half % 32 == 0 else 16
        m_ref, f_ref, s_ref = refs

        def step(i, carry):
            clip = factor_ref[0:1, :]
            at = pl.ds(pl.multiple_of(core_index * half + i * rows, rows), rows)
            for c in range(chunks):
                cols = pl.ds(c * LANES, LANES)
                grad = clip * sums[c, core_index, pl.ds(pl.multiple_of(base + i * rows, 8), rows), :]
                m, f, s = adamw(grad, m_ref[at, cols], f_ref[at, cols], s_ref[at, cols], 0.01)
                m_ref[at, cols] = m
                f_ref[at, cols] = f
                s_ref[at, cols] = s
                weights[at, cols] = m.astype(jnp.bfloat16)
            return carry

        lax.fori_loop(0, half // rows, step, 0)

    for core_index in range(2):
        update((state_em, state_ef, state_es), local_ew, e_half, 0, core_index)
    norm_cols = norm_m.shape[1]
    mine = norm_acc[len(all_bits), :, 0:norm_cols]
    for s in range(1, shards):
        mine = jnp.where(shard == s, norm_acc[len(all_bits), :, s * norm_cols:(s + 1) * norm_cols], mine)
    m, f, s = adamw(factor_ref[0:1, 0:1] * mine, norm_m[...], norm_f[...], norm_s[...], 0.0)
    out_nm[...] = m
    out_nf[...] = f
    out_ns[...] = s
    norm_w[shard] = m

    width = half_chunks * LANES
    streams = [(0, width, ascending)]
    if width < chunks * LANES:
        streams.append((width, chunks * LANES - width, ascending[::-1]))

    def e_rows(zmask, mask):
        start = flipped(shard, zmask) * (2 * e_half) + core * e_half + flipped(sub, mask) * piece
        return pl.ds(pl.multiple_of(start, 16), piece)

    def e_half_rows(zmask):
        start = flipped(shard, zmask) * (2 * e_half) + core * e_half
        return pl.ds(pl.multiple_of(start, 16), e_half)

    def p_rows(zmask):
        start = flipped(shard, zmask) * (2 * p_half) + core * p_half
        return pl.ds(pl.multiple_of(start, 16), p_half)

    def send_e(zmask, lo, size, bit):
        cols = pl.ds(lo, size)
        if zmask == 0:
            at = pl.ds(pl.multiple_of(core * e_half + sub * piece, 16), piece)
            src = local_ew.at[at, cols]
        else:
            src = out_ew.at[e_rows(zmask, 0), cols]
        return send(src, out_ew.at[e_rows(zmask, 0), cols], "shard", bit)

    def send_p(zmask, bit):
        if zmask == 0:
            src = local_pw.at[pl.ds(pl.multiple_of(core * p_half, 16), p_half)]
        else:
            src = out_pw.at[p_rows(zmask)]
        return send(src, out_pw.at[p_rows(zmask)], "shard", bit)

    def send_n(zmask, bit):
        ref = norm_w.at[flipped(shard, zmask)]
        return send(ref, ref, "shard", bit)

    bits = list(reversed(range(shard_bits)))
    held = [0]
    pending = [[send_e(0, lo, size, bits[0])] for lo, size, _ in streams]
    for core_index in range(2):
        update((state_pm, state_pf, state_ps), local_pw, p_half, e_half, core_index)
    outs = [
        local(src, dst)
        for src, dst in (
            (local_ew, out_ew.at[pl.ds(pl.multiple_of(shard * (2 * e_half), 16), 2 * e_half)]),
            (local_pw, out_pw.at[pl.ds(pl.multiple_of(shard * (2 * p_half), 16), 2 * p_half)]),
            (state_em, out_em), (state_ef, out_ef), (state_es, out_es),
            (state_pm, out_pm), (state_pf, out_pf), (state_ps, out_ps),
        )
    ]
    proj_pending = [send_p(0, bits[0])]
    norm_pending = [send_n(0, bits[0])]
    held = [0, 1 << bits[0]]
    for b in bits[1:]:
        for i, (lo, size, _) in enumerate(streams):
            for copy in pending[i]:
                copy.wait_recv()
            pending[i] = [send_e(z, lo, size, b) for z in held]
        for copy in proj_pending + norm_pending:
            copy.wait_recv()
        proj_pending = [send_p(z, b) for z in held]
        norm_pending = [send_n(z, b) for z in held]
        held = held + [z | 1 << b for z in held]

    masks = [[0] for _ in streams]
    for t in range(rep_bits - 1):
        for i, (lo, size, order) in enumerate(streams):
            for copy in pending[i]:
                copy.wait_recv()
            pending[i] = []
            for m in masks[i]:
                for z in range(1, shards):
                    ref = out_ew.at[e_rows(z, m), pl.ds(lo, size)]
                    pending[i].append(send(ref, ref, "rep", order[t]))
            masks[i] = masks[i] + [m | 1 << (order[t] - 1) for m in masks[i]]
    for copy in proj_pending + norm_pending:
        copy.wait_recv()
    last = []
    for z in range(1, shards):
        ref = out_pw.at[p_rows(z)]
        last.append(send(ref, ref, "rep", 0))
    for i, (lo, size, _) in enumerate(streams):
        for copy in pending[i]:
            copy.wait_recv()
        for z in range(1, shards):
            ref = out_ew.at[e_half_rows(z), pl.ds(lo, size)]
            last.append(send(ref, ref, "rep", 0))
    out_nw[...] = norm_w[...]
    for copy in last:
        copy.wait_recv()
    for copy in sends:
        copy.wait_send()
    for copy in outs:
        copy.wait()


def shards_fn(
    reps,
    shards,
    grad_embed, grad_proj, grad_norms,
    embed_master, embed_first, embed_second,
    proj_master, proj_first, proj_second,
    norm_master, norm_first, norm_second,
):
    embed_rows, width = grad_embed.shape[2:]
    proj_rows = grad_proj.shape[2]
    norm_rows, norm_cols = norm_master.shape
    chunks = width // LANES
    e_half = embed_rows // shards // 2
    p_half = proj_rows // shards // 2
    subs = reps // 2
    unit = 8 * subs
    half_rows = -(-(e_half + p_half) // unit) * unit
    block = half_rows // subs
    entry_count = float((embed_rows + proj_rows + norm_rows) * width)
    rep_bits = reps.bit_length() - 1
    shard_bits = shards.bit_length() - 1
    all_bits = rep_bits + shard_bits
    n_dims = all_bits - 1
    f32, bf16 = jnp.float32, jnp.bfloat16
    n_streams = 2 if chunks > 1 else 1
    copies = 2 * chunks + 2 * all_bits + chunks * n_dims + chunks * subs
    copies += (n_streams + 2) * (shards - 1)
    copies += n_streams * (shards - 1) * subs + (shards - 1)
    plan = (reps, shards, chunks, e_half, p_half, half_rows, entry_count)
    any_spec = pl.BlockSpec(memory_space=pl.ANY)
    vmem_spec = pl.BlockSpec(memory_space=pltpu.VMEM)
    e_part, p_part = (2 * e_half, width), (2 * p_half, width)
    landed = [
        pltpu.VMEM((chunks,) + (2,) * (n_dims - 1 - k) + (block, LANES), f32) for k in range(n_dims)
    ]
    outs = pl.pallas_call(
        functools.partial(kernel, plan),
        out_shape=(
            [jax.ShapeDtypeStruct(e_part, f32)] * 3
            + [jax.ShapeDtypeStruct((embed_rows, width), bf16)]
            + [jax.ShapeDtypeStruct(p_part, f32)] * 3
            + [jax.ShapeDtypeStruct((proj_rows, width), bf16)]
            + [jax.ShapeDtypeStruct((norm_rows, norm_cols), f32)] * 3
            + [jax.ShapeDtypeStruct((shards, norm_rows, norm_cols), f32)]
        ),
        in_specs=[any_spec] * 2 + [vmem_spec] + [any_spec] * 6 + [vmem_spec] * 3,
        out_specs=[any_spec] * 8 + [vmem_spec] * 4,
        scratch_shapes=[
            pltpu.VMEM((chunks, shards, e_half, LANES), bf16),
            pltpu.VMEM((chunks, shards, p_half, LANES), bf16),
            pltpu.VMEM((chunks, shards, e_half, LANES), bf16),
            pltpu.VMEM((chunks, shards, p_half, LANES), bf16),
            pltpu.VMEM((chunks,) + (2,) * n_dims + (block, LANES), f32),
            pltpu.VMEM((chunks, 2, half_rows, LANES), f32),
            pltpu.VMEM(e_part, f32), pltpu.VMEM(e_part, f32), pltpu.VMEM(e_part, f32),
            pltpu.VMEM(p_part, f32), pltpu.VMEM(p_part, f32), pltpu.VMEM(p_part, f32),
            pltpu.VMEM(e_part, bf16), pltpu.VMEM(p_part, bf16),
            pltpu.VMEM((all_bits + 1, norm_rows, width), f32),
            pltpu.VMEM((all_bits, norm_rows, width), f32),
            pltpu.VMEM((shards, norm_rows, norm_cols), f32),
            pltpu.VMEM((all_bits + 1, 8, LANES), f32),
            pltpu.VMEM((all_bits, 8, LANES), f32),
            pltpu.VMEM((8, LANES), f32),
        ]
        + landed
        + [
            pltpu.SemaphoreType.DMA((copies,)),
            pltpu.SemaphoreType.DMA((copies,)),
            pltpu.SemaphoreType.DMA((2 * chunks + 14,)),
        ],
        compiler_params=pltpu.CompilerParams(
            collective_id=0, has_side_effects=True, vmem_limit_bytes=58 * 1024 * 1024
        ),
    )(
        grad_embed.reshape(shards, 2, e_half, width),
        grad_proj.reshape(shards, 2, p_half, width),
        grad_norms[0, 0],
        embed_master, embed_first, embed_second,
        proj_master, proj_first, proj_second,
        norm_master, norm_first, norm_second,
    )
    norm_weights = outs[11].astype(bf16).transpose(1, 0, 2).reshape(norm_rows, width)
    return tuple(outs[:11]) + (norm_weights,)


def solution(mesh):
    grad, part, whole = P("rep", "shard", None, None), P("shard", None), P()
    cols = P(None, "shard")
    return jax.shard_map(
        functools.partial(shards_fn, mesh.shape["rep"], mesh.shape["shard"]),
        mesh=mesh,
        in_specs=(grad,) * 3 + (part,) * 6 + (cols,) * 3,
        out_specs=(part,) * 3 + (whole,) + (part,) * 3 + (whole,) + (cols,) * 3 + (whole,),
        check_vma=False,
    )
```

```python
import functools

import jax
import jax.numpy as jnp
from jax import lax
from jax.experimental import pallas as pl
from jax.experimental.pallas import tpu as pltpu
from jax.sharding import PartitionSpec as P

beta_one = 0.9
beta_two = 0.95
adam_step = 10.0
adam_eps = 1e-08
learning_rate = 0.002
clip_rms = 1.0
LANES = 128
MESH = pl.DeviceIdType.MESH


def adamw(gradient, master, first, second, weight_decay):
    corr_one = 1.0 - beta_one**adam_step
    corr_two = 1.0 - beta_two**adam_step
    first_new = beta_one * first + (1.0 - beta_one) * gradient
    second_new = beta_two * second + (1.0 - beta_two) * gradient * gradient
    direction = (
        first_new * (1.0 / corr_one) / (jnp.sqrt(second_new * (1.0 / corr_two)) + adam_eps)
        + weight_decay * master
    )
    master_new = master - learning_rate * direction
    return (master_new, first_new, second_new)


def bit_of(index, bit):
    return lax.rem(lax.div(index, 1 << bit), 2)


def flipped(index, mask):
    bit = 0
    out = index
    while mask >> bit:
        if (mask >> bit) & 1:
            out = out + (1 - 2 * bit_of(index, bit)) * (1 << bit)
        bit += 1
    return out


def tile_sum(values):
    return jnp.sum(values.reshape(values.shape[0] // 8, 8, LANES), axis=0)


def kernel(
    plan,
    grad_embed, grad_proj, grad_norm,
    embed_m, embed_f, embed_s, proj_m, proj_f, proj_s, norm_m, norm_f, norm_s,
    out_em, out_ef, out_es, out_ew, out_pm, out_pf, out_ps, out_pw,
    out_nm, out_nf, out_ns, out_nw,
    own_e, own_p, got_e, got_p, work, sums,
    state_em, state_ef, state_es, state_pm, state_pf, state_ps, local_ew, local_pw,
    norm_acc, norm_got, norm_w, square_acc, square_got, factor_ref,
    *rest,
):
    reps, shards, chunks, e_half, p_half, half_rows, entry_count = plan
    send_sem, recv_sem, local_sem = rest[-3:]
    landed = rest[:-3]
    rep_bits = reps.bit_length() - 1
    shard_bits = shards.bit_length() - 1
    subs = reps // 2
    block = half_rows // subs
    piece = e_half // subs
    rep = lax.axis_index("rep")
    shard = lax.axis_index("shard")
    core = lax.rem(rep, 2)
    sub = lax.div(rep, 2)
    where = {"rep": rep, "shard": shard}
    all_bits = [("rep", b) for b in range(rep_bits)] + [("shard", b) for b in range(shard_bits)]

    sends = []
    locals_ = []

    def send(src, dst, axis, bit):
        i = len(sends)
        copy = pltpu.make_async_remote_copy(
            src_ref=src, dst_ref=dst, send_sem=send_sem.at[i], recv_sem=recv_sem.at[i],
            device_id={axis: flipped(where[axis], 1 << bit)}, device_id_type=MESH,
        )
        copy.start()
        sends.append(copy)
        return copy

    def local(src, dst):
        copy = pltpu.make_async_copy(src, dst, local_sem.at[len(locals_)])
        copy.start()
        locals_.append(copy)
        return copy

    ascending = list(range(1, rep_bits))
    half_chunks = max(chunks // 2, 1)

    def rep_order(c):
        return ascending if c < half_chunks else ascending[::-1]

    turn = []
    for i in range(half_chunks):
        turn += [c for c in (i, i + half_chunks) if c < chunks]

    own = {}
    for c in turn:
        cols = pl.ds(c * LANES, LANES)
        own[c] = (
            local(grad_embed.at[:, core, :, cols], own_e.at[c]),
            local(grad_proj.at[:, core, :, cols], own_p.at[c]),
        )
    barrier = pltpu.get_barrier_semaphore()
    for axis, b in all_bits:
        pl.semaphore_signal(
            barrier, inc=1, device_id={axis: flipped(where[axis], 1 << b)}, device_id_type=MESH
        )
    pl.semaphore_wait(barrier, len(all_bits))

    other = 1 - core
    first_hop = {}
    for c in turn:
        cols = pl.ds(c * LANES, LANES)
        first_hop[c] = (
            send(grad_embed.at[:, other, :, cols], got_e.at[c], "rep", 0),
            send(grad_proj.at[:, other, :, cols], got_p.at[c], "rep", 0),
        )
    states = [
        local(src, dst)
        for src, dst in (
            (embed_m, state_em), (embed_f, state_ef), (embed_s, state_es),
            (proj_m, state_pm), (proj_f, state_pf), (proj_s, state_ps),
        )
    ]

    norm_acc[0] = grad_norm[...].astype(jnp.float32)
    norm_copy = send(norm_acc.at[0], norm_got.at[0], *all_bits[0])
    norm_round = 0

    dims = [("shard", b) for b in reversed(range(shard_bits))]
    dims += [("rep", b) for b in reversed(range(1, rep_bits))]

    def region(c, done, dim=None, value=None):
        index = [c]
        for d in dims:
            if d == dim:
                index.append(value)
            elif d in done:
                index.append(bit_of(where[d[0]], d[1]))
            else:
                index.append(slice(None))
        return tuple(index)

    def stage_order(c):
        reps_part = [("rep", b) for b in rep_order(c)]
        first = len(reps_part) if c % half_chunks == half_chunks - 1 else 1
        shard_part = [("shard", b) for b in range(shard_bits)]
        return reps_part[:first] + shard_part + reps_part[first:]

    hops = {}

    def start_hop(c, k):
        order = stage_order(c)
        dim = order[k]
        theirs = 1 - bit_of(where[dim[0]], dim[1])
        hops[c] = send(work.at[region(c, order[:k], dim, theirs)], landed[k].at[c], *dim)

    for c in turn:
        for copy in own[c]:
            copy.wait()
        for copy in first_hop[c]:
            copy.wait_recv()
        for s in range(shards):
            parts = [
                own_e[c, s].astype(jnp.float32) + got_e[c, s].astype(jnp.float32),
                own_p[c, s].astype(jnp.float32) + got_p[c, s].astype(jnp.float32),
            ]
            pad = half_rows - e_half - p_half
            if pad:
                parts.append(jnp.zeros((pad, LANES), jnp.float32))
            slab = jnp.concatenate(parts, axis=0)
            index = (c,) + tuple((s >> b) & 1 for b in reversed(range(shard_bits)))
            work[index] = slab.reshape((2,) * (rep_bits - 1) + (block, LANES))
        start_hop(c, 0)

    gathers = {}
    masks_of = {c: [0] for c in turn}

    def sub_rows(mask):
        return pl.ds(pl.multiple_of(flipped(sub, mask) * block, 8), block)

    def start_gather(c, t):
        order = rep_order(c)[::-1]
        gathers[c] = []
        if t < len(order):
            for mask in masks_of[c]:
                ref = sums.at[c, core, sub_rows(mask)]
                gathers[c].append(send(ref, ref, "rep", order[t]))
            masks_of[c] = masks_of[c] + [m | 1 << (order[t] - 1) for m in masks_of[c]]
        else:
            ref = sums.at[c, core]
            gathers[c].append(send(ref, ref, "rep", 0))

    def advance_norm(current):
        copy, done = current
        if copy is None:
            return current
        copy.wait_recv()
        norm_acc[done + 1] = norm_acc[done] + norm_got[done]
        done += 1
        if done < len(all_bits):
            return send(norm_acc.at[done], norm_got.at[done], *all_bits[done]), done
        return None, done

    def advance_square(current):
        copy, done = current
        if copy is None:
            return current
        copy.wait_recv()
        square_acc[done + 1] = square_acc[done] + square_got[done]
        done += 1
        if done < len(all_bits):
            return send(square_acc.at[done], square_got.at[done], *all_bits[done]), done
        return None, done

    n_dims = len(dims)
    events = sorted(
        (1.5 * (c % half_chunks) + k, k, turn.index(c), c)
        for c in turn for k in range(n_dims + rep_bits - 1)
    )
    norm_state, square_state = (norm_copy, 0), (None, 0)
    squares = jnp.zeros((8, LANES), jnp.float32)
    reduced = 0
    for step, (_, k, _, c) in enumerate(events):
        if k < n_dims:
            order = stage_order(c)
            dim = order[k]
            hops[c].wait_recv()
            index = region(c, order[:k], dim, bit_of(where[dim[0]], dim[1]))
            total = work[index] + landed[k][c]
            if k + 1 < n_dims:
                work[index] = total
                start_hop(c, k + 1)
            else:
                sums[c, core, sub_rows(0), :] = total
                start_gather(c, 0)
                squares = squares + tile_sum(total * total)
                reduced += 1
                if reduced == chunks:
                    square_acc[0] = squares
                    square_state = (send(square_acc.at[0], square_got.at[0], *all_bits[0]), 0)
        else:
            for copy in gathers[c]:
                copy.wait_recv()
            start_gather(c, k - n_dims + 1)
            if reduced == chunks:
                square_state = advance_square(square_state)
        if step % 3 == 2:
            norm_state = advance_norm(norm_state)
    while norm_state[0] is not None:
        norm_state = advance_norm(norm_state)
    while square_state[0] is not None:
        square_state = advance_square(square_state)
    for c in turn:
        for copy in gathers[c]:
            copy.wait_recv()

    norm_sum = norm_acc[len(all_bits)]
    total = jnp.sum(square_acc[len(all_bits)], axis=(0, 1), keepdims=True)
    total = total + jnp.sum(norm_sum * norm_sum, axis=(0, 1), keepdims=True)
    rms = jnp.sqrt(total / entry_count)
    factor = jnp.minimum(jnp.float32(1.0), clip_rms / (rms + 1e-06))
    factor_ref[...] = jnp.broadcast_to(factor, factor_ref.shape)
    for copy in states:
        copy.wait()

    def update(refs, weights, half, base, core_index, first, count):
        rows = 32 if count % 32 == 0 else 16
        m_ref, f_ref, s_ref = refs

        def step(i, carry):
            clip = factor_ref[0:1, :]
            begin = first + i * rows
            at = pl.ds(pl.multiple_of(core_index * half + begin, rows), rows)
            for c in range(chunks):
                cols = pl.ds(c * LANES, LANES)
                grad = clip * sums[c, core_index, pl.ds(pl.multiple_of(base + begin, 8), rows), :]
                m, f, s = adamw(grad, m_ref[at, cols], f_ref[at, cols], s_ref[at, cols], 0.01)
                m_ref[at, cols] = m
                f_ref[at, cols] = f
                s_ref[at, cols] = s
                weights[at, cols] = m.astype(jnp.bfloat16)
            return carry

        lax.fori_loop(0, count // rows, step, 0)

    def update_e(core_index, first, count):
        update((state_em, state_ef, state_es), local_ew, e_half, 0, core_index, first, count)

    def update_p(core_index):
        update((state_pm, state_pf, state_ps), local_pw, p_half, e_half, core_index, 0, p_half)

    width = half_chunks * LANES
    streams = [(0, width, ascending)]
    if width < chunks * LANES:
        streams.append((width, chunks * LANES - width, ascending[::-1]))

    def e_rows(zmask, mask):
        start = flipped(shard, zmask) * (2 * e_half) + core * e_half + flipped(sub, mask) * piece
        return pl.ds(pl.multiple_of(start, 16), piece)

    def e_half_rows(zmask):
        start = flipped(shard, zmask) * (2 * e_half) + core * e_half
        return pl.ds(pl.multiple_of(start, 16), e_half)

    def p_rows(zmask):
        start = flipped(shard, zmask) * (2 * p_half) + core * p_half
        return pl.ds(pl.multiple_of(start, 16), p_half)

    def send_e(zmask, lo, size, bit):
        cols = pl.ds(lo, size)
        if zmask == 0:
            at = pl.ds(pl.multiple_of(core * e_half + sub * piece, 16), piece)
            src = local_ew.at[at, cols]
        else:
            src = out_ew.at[e_rows(zmask, 0), cols]
        return send(src, out_ew.at[e_rows(zmask, 0), cols], "shard", bit)

    def send_p(zmask, bit):
        if zmask == 0:
            src = local_pw.at[pl.ds(pl.multiple_of(core * p_half, 16), p_half)]
        else:
            src = out_pw.at[p_rows(zmask)]
        return send(src, out_pw.at[p_rows(zmask)], "shard", bit)

    def send_n(zmask, bit):
        ref = norm_w.at[flipped(shard, zmask)]
        return send(ref, ref, "shard", bit)

    bits = list(reversed(range(shard_bits)))
    update_e(core, sub * piece, piece)
    pending = [[send_e(0, lo, size, bits[0])] for lo, size, _ in streams]
    norm_cols = norm_m.shape[1]
    mine = norm_acc[len(all_bits), :, 0:norm_cols]
    for s in range(1, shards):
        mine = jnp.where(shard == s, norm_acc[len(all_bits), :, s * norm_cols:(s + 1) * norm_cols], mine)
    m, f, s = adamw(factor_ref[0:1, 0:1] * mine, norm_m[...], norm_f[...], norm_s[...], 0.0)
    out_nm[...] = m
    out_nf[...] = f
    out_ns[...] = s
    norm_w[shard] = m
    norm_pending = [send_n(0, bits[0])]
    update_p(core)
    rest_parts = [functools.partial(update_p, other)]
    rest_parts += [
        functools.partial(update_e, core, flipped(sub, m) * piece, piece) for m in range(1, subs)
    ]
    rest_parts.append(functools.partial(update_e, other, 0, e_half))
    rest_parts.reverse()
    rest_parts.pop(0)()
    held = [0, 1 << bits[0]]
    proj_pending = []
    for n, b in enumerate(bits[1:]):
        for i, (lo, size, _) in enumerate(streams):
            for copy in pending[i]:
                copy.wait_recv()
            pending[i] = [send_e(z, lo, size, b) for z in held]
        for copy in norm_pending:
            copy.wait_recv()
        norm_pending = [send_n(z, b) for z in held]
        if n == 0:
            proj_pending = [send_p(0, bits[0])]
        held = held + [z | 1 << b for z in held]
    if not proj_pending:
        proj_pending = [send_p(0, bits[0])]
    for part in rest_parts:
        part()
    outs = [
        local(src, dst)
        for src, dst in (
            (local_ew, out_ew.at[pl.ds(pl.multiple_of(shard * (2 * e_half), 16), 2 * e_half)]),
            (local_pw, out_pw.at[pl.ds(pl.multiple_of(shard * (2 * p_half), 16), 2 * p_half)]),
            (state_em, out_em), (state_ef, out_ef), (state_es, out_es),
            (state_pm, out_pm), (state_pf, out_pf), (state_ps, out_ps),
        )
    ]
    proj_held = [0, 1 << bits[0]]
    proj_bits = bits[1:]

    def advance_proj():
        nonlocal proj_pending, proj_held, proj_bits
        if proj_bits:
            b, proj_bits = proj_bits[0], proj_bits[1:]
            for copy in proj_pending:
                copy.wait_recv()
            proj_pending = [send_p(z, b) for z in proj_held]
            proj_held = proj_held + [z | 1 << b for z in proj_held]

    masks = [[0] for _ in streams]
    for t in range(rep_bits - 1):
        for i, (lo, size, order) in enumerate(streams):
            for copy in pending[i]:
                copy.wait_recv()
            pending[i] = []
            for m in masks[i]:
                for z in range(1, shards):
                    ref = out_ew.at[e_rows(z, m), pl.ds(lo, size)]
                    pending[i].append(send(ref, ref, "rep", order[t]))
            masks[i] = masks[i] + [m | 1 << (order[t] - 1) for m in masks[i]]
        advance_proj()
    while proj_bits:
        advance_proj()
    for copy in proj_pending + norm_pending:
        copy.wait_recv()
    last = []
    for z in range(1, shards):
        ref = out_pw.at[p_rows(z)]
        last.append(send(ref, ref, "rep", 0))
    for i, (lo, size, _) in enumerate(streams):
        for copy in pending[i]:
            copy.wait_recv()
        for z in range(1, shards):
            ref = out_ew.at[e_half_rows(z), pl.ds(lo, size)]
            last.append(send(ref, ref, "rep", 0))
    out_nw[...] = norm_w[...]
    for copy in last:
        copy.wait_recv()
    for copy in sends:
        copy.wait_send()
    for copy in outs:
        copy.wait()


def shards_fn(
    reps,
    shards,
    grad_embed, grad_proj, grad_norms,
    embed_master, embed_first, embed_second,
    proj_master, proj_first, proj_second,
    norm_master, norm_first, norm_second,
):
    embed_rows, width = grad_embed.shape[2:]
    proj_rows = grad_proj.shape[2]
    norm_rows, norm_cols = norm_master.shape
    chunks = width // LANES
    e_half = embed_rows // shards // 2
    p_half = proj_rows // shards // 2
    subs = reps // 2
    unit = 8 * subs
    half_rows = -(-(e_half + p_half) // unit) * unit
    block = half_rows // subs
    entry_count = float((embed_rows + proj_rows + norm_rows) * width)
    rep_bits = reps.bit_length() - 1
    shard_bits = shards.bit_length() - 1
    all_bits = rep_bits + shard_bits
    n_dims = all_bits - 1
    f32, bf16 = jnp.float32, jnp.bfloat16
    n_streams = 2 if chunks > 1 else 1
    copies = 2 * chunks + 2 * all_bits + chunks * n_dims + chunks * subs
    copies += (n_streams + 2) * (shards - 1)
    copies += n_streams * (shards - 1) * subs + (shards - 1)
    plan = (reps, shards, chunks, e_half, p_half, half_rows, entry_count)
    any_spec = pl.BlockSpec(memory_space=pl.ANY)
    vmem_spec = pl.BlockSpec(memory_space=pltpu.VMEM)
    e_part, p_part = (2 * e_half, width), (2 * p_half, width)
    landed = [
        pltpu.VMEM((chunks,) + (2,) * (n_dims - 1 - k) + (block, LANES), f32) for k in range(n_dims)
    ]
    outs = pl.pallas_call(
        functools.partial(kernel, plan),
        out_shape=(
            [jax.ShapeDtypeStruct(e_part, f32)] * 3
            + [jax.ShapeDtypeStruct((embed_rows, width), bf16)]
            + [jax.ShapeDtypeStruct(p_part, f32)] * 3
            + [jax.ShapeDtypeStruct((proj_rows, width), bf16)]
            + [jax.ShapeDtypeStruct((norm_rows, norm_cols), f32)] * 3
            + [jax.ShapeDtypeStruct((shards, norm_rows, norm_cols), f32)]
        ),
        in_specs=[any_spec] * 2 + [vmem_spec] + [any_spec] * 6 + [vmem_spec] * 3,
        out_specs=[any_spec] * 8 + [vmem_spec] * 4,
        scratch_shapes=[
            pltpu.VMEM((chunks, shards, e_half, LANES), bf16),
            pltpu.VMEM((chunks, shards, p_half, LANES), bf16),
            pltpu.VMEM((chunks, shards, e_half, LANES), bf16),
            pltpu.VMEM((chunks, shards, p_half, LANES), bf16),
            pltpu.VMEM((chunks,) + (2,) * n_dims + (block, LANES), f32),
            pltpu.VMEM((chunks, 2, half_rows, LANES), f32),
            pltpu.VMEM(e_part, f32), pltpu.VMEM(e_part, f32), pltpu.VMEM(e_part, f32),
            pltpu.VMEM(p_part, f32), pltpu.VMEM(p_part, f32), pltpu.VMEM(p_part, f32),
            pltpu.VMEM(e_part, bf16), pltpu.VMEM(p_part, bf16),
            pltpu.VMEM((all_bits + 1, norm_rows, width), f32),
            pltpu.VMEM((all_bits, norm_rows, width), f32),
            pltpu.VMEM((shards, norm_rows, norm_cols), f32),
            pltpu.VMEM((all_bits + 1, 8, LANES), f32),
            pltpu.VMEM((all_bits, 8, LANES), f32),
            pltpu.VMEM((8, LANES), f32),
        ]
        + landed
        + [
            pltpu.SemaphoreType.DMA((copies,)),
            pltpu.SemaphoreType.DMA((copies,)),
            pltpu.SemaphoreType.DMA((2 * chunks + 14,)),
        ],
        compiler_params=pltpu.CompilerParams(
            collective_id=0, has_side_effects=True, vmem_limit_bytes=58 * 1024 * 1024
        ),
    )(
        grad_embed.reshape(shards, 2, e_half, width),
        grad_proj.reshape(shards, 2, p_half, width),
        grad_norms[0, 0],
        embed_master, embed_first, embed_second,
        proj_master, proj_first, proj_second,
        norm_master, norm_first, norm_second,
    )
    norm_weights = outs[11].astype(bf16).transpose(1, 0, 2).reshape(norm_rows, width)
    return tuple(outs[:11]) + (norm_weights,)


def solution(mesh):
    grad, part, whole = P("rep", "shard", None, None), P("shard", None), P()
    cols = P(None, "shard")
    return jax.shard_map(
        functools.partial(shards_fn, mesh.shape["rep"], mesh.shape["shard"]),
        mesh=mesh,
        in_specs=(grad,) * 3 + (part,) * 6 + (cols,) * 3,
        out_specs=(part,) * 3 + (whole,) + (part,) * 3 + (whole,) + (cols,) * 3 + (whole,),
        check_vma=False,
    )
```

```python
import functools

import jax
import jax.numpy as jnp
from jax import lax
from jax.experimental import pallas as pl
from jax.experimental.pallas import tpu as pltpu
from jax.sharding import PartitionSpec as P

beta_one = 0.9
beta_two = 0.95
adam_step = 10.0
adam_eps = 1e-08
learning_rate = 0.002
clip_rms = 1.0
LANES = 128
MESH = pl.DeviceIdType.MESH


def adamw(gradient, master, first, second, weight_decay):
    corr_one = 1.0 - beta_one**adam_step
    corr_two = 1.0 - beta_two**adam_step
    first_new = beta_one * first + (1.0 - beta_one) * gradient
    second_new = beta_two * second + (1.0 - beta_two) * gradient * gradient
    direction = (
        first_new * (1.0 / corr_one) / (jnp.sqrt(second_new * (1.0 / corr_two)) + adam_eps)
        + weight_decay * master
    )
    master_new = master - learning_rate * direction
    return (master_new, first_new, second_new)


def bit_of(index, bit):
    return lax.rem(lax.div(index, 1 << bit), 2)


def flipped(index, mask):
    bit = 0
    out = index
    while mask >> bit:
        if (mask >> bit) & 1:
            out = out + (1 - 2 * bit_of(index, bit)) * (1 << bit)
        bit += 1
    return out


def tile_sum(values):
    return jnp.sum(values.reshape(values.shape[0] // 8, 8, LANES), axis=0)


def kernel(
    plan,
    grad_embed, grad_proj, grad_norm,
    embed_m, embed_f, embed_s, proj_m, proj_f, proj_s, norm_m, norm_f, norm_s,
    out_em, out_ef, out_es, out_ew, out_pm, out_pf, out_ps, out_pw,
    out_nm, out_nf, out_ns, out_nw,
    own_e, own_p, got_e, got_p, work, sums,
    state_em, state_ef, state_es, state_pm, state_pf, state_ps, local_ew, local_pw,
    norm_acc, norm_got, norm_w, square_acc, square_got, factor_ref,
    *rest,
):
    reps, shards, chunks, e_half, p_half, half_rows, entry_count = plan
    send_sem, recv_sem, local_sem = rest[-3:]
    landed = rest[:-3]
    rep_bits = reps.bit_length() - 1
    shard_bits = shards.bit_length() - 1
    subs = reps // 2
    block = half_rows // subs
    piece = e_half // subs
    rep = lax.axis_index("rep")
    shard = lax.axis_index("shard")
    core = lax.rem(rep, 2)
    sub = lax.div(rep, 2)
    where = {"rep": rep, "shard": shard}
    all_bits = [("rep", b) for b in range(rep_bits)] + [("shard", b) for b in range(shard_bits)]

    sends = []
    locals_ = []

    def send(src, dst, axis, bit):
        i = len(sends)
        copy = pltpu.make_async_remote_copy(
            src_ref=src, dst_ref=dst, send_sem=send_sem.at[i], recv_sem=recv_sem.at[i],
            device_id={axis: flipped(where[axis], 1 << bit)}, device_id_type=MESH,
        )
        copy.start()
        sends.append(copy)
        return copy

    def local(src, dst):
        copy = pltpu.make_async_copy(src, dst, local_sem.at[len(locals_)])
        copy.start()
        locals_.append(copy)
        return copy

    ascending = list(range(1, rep_bits))
    half_chunks = max(chunks // 2, 1)

    def rep_order(c):
        return ascending if c < half_chunks else ascending[::-1]

    turn = []
    for i in range(half_chunks):
        turn += [c for c in (i, i + half_chunks) if c < chunks]

    own = {}
    for c in turn:
        cols = pl.ds(c * LANES, LANES)
        own[c] = (
            local(grad_embed.at[:, core, :, cols], own_e.at[c]),
            local(grad_proj.at[:, core, :, cols], own_p.at[c]),
        )
    barrier = pltpu.get_barrier_semaphore()
    for axis, b in all_bits:
        pl.semaphore_signal(
            barrier, inc=1, device_id={axis: flipped(where[axis], 1 << b)}, device_id_type=MESH
        )
    pl.semaphore_wait(barrier, len(all_bits))

    other = 1 - core
    first_hop = {}
    for c in turn:
        cols = pl.ds(c * LANES, LANES)
        first_hop[c] = (
            send(grad_embed.at[:, other, :, cols], got_e.at[c], "rep", 0),
            send(grad_proj.at[:, other, :, cols], got_p.at[c], "rep", 0),
        )
    states = [
        local(src, dst)
        for src, dst in (
            (embed_m, state_em), (embed_f, state_ef), (embed_s, state_es),
            (proj_m, state_pm), (proj_f, state_pf), (proj_s, state_ps),
        )
    ]

    norm_acc[0] = grad_norm[...].astype(jnp.float32)
    norm_copy = send(norm_acc.at[0], norm_got.at[0], *all_bits[0])
    norm_round = 0

    dims = [("shard", b) for b in reversed(range(shard_bits))]
    dims += [("rep", b) for b in reversed(range(1, rep_bits))]

    def region(c, done, dim=None, value=None):
        index = [c]
        for d in dims:
            if d == dim:
                index.append(value)
            elif d in done:
                index.append(bit_of(where[d[0]], d[1]))
            else:
                index.append(slice(None))
        return tuple(index)

    def stage_order(c):
        reps_part = [("rep", b) for b in rep_order(c)]
        first = len(reps_part) if c % half_chunks == half_chunks - 1 else 1
        shard_part = [("shard", b) for b in range(shard_bits)]
        return reps_part[:first] + shard_part + reps_part[first:]

    hops = {}

    def start_hop(c, k):
        order = stage_order(c)
        dim = order[k]
        theirs = 1 - bit_of(where[dim[0]], dim[1])
        hops[c] = send(work.at[region(c, order[:k], dim, theirs)], landed[k].at[c], *dim)

    for c in turn:
        for copy in own[c]:
            copy.wait()
        for copy in first_hop[c]:
            copy.wait_recv()
        for s in range(shards):
            parts = [
                own_e[c, s].astype(jnp.float32) + got_e[c, s].astype(jnp.float32),
                own_p[c, s].astype(jnp.float32) + got_p[c, s].astype(jnp.float32),
            ]
            pad = half_rows - e_half - p_half
            if pad:
                parts.append(jnp.zeros((pad, LANES), jnp.float32))
            slab = jnp.concatenate(parts, axis=0)
            index = (c,) + tuple((s >> b) & 1 for b in reversed(range(shard_bits)))
            work[index] = slab.reshape((2,) * (rep_bits - 1) + (block, LANES))
        start_hop(c, 0)

    gathers = {}
    masks_of = {c: [0] for c in turn}

    def sub_rows(mask):
        return pl.ds(pl.multiple_of(flipped(sub, mask) * block, 8), block)

    def start_gather(c, t):
        order = rep_order(c)[::-1]
        gathers[c] = []
        if t < len(order):
            for mask in masks_of[c]:
                ref = sums.at[c, core, sub_rows(mask)]
                gathers[c].append(send(ref, ref, "rep", order[t]))
            masks_of[c] = masks_of[c] + [m | 1 << (order[t] - 1) for m in masks_of[c]]
        else:
            ref = sums.at[c, core]
            gathers[c].append(send(ref, ref, "rep", 0))

    def advance_norm(current):
        copy, done = current
        if copy is None:
            return current
        copy.wait_recv()
        norm_acc[done + 1] = norm_acc[done] + norm_got[done]
        done += 1
        if done < len(all_bits):
            return send(norm_acc.at[done], norm_got.at[done], *all_bits[done]), done
        return None, done

    def advance_square(current):
        copy, done = current
        if copy is None:
            return current
        copy.wait_recv()
        square_acc[done + 1] = square_acc[done] + square_got[done]
        done += 1
        if done < len(all_bits):
            return send(square_acc.at[done], square_got.at[done], *all_bits[done]), done
        return None, done

    n_dims = len(dims)
    events = sorted(
        (1.5 * (c % half_chunks) + k, k, turn.index(c), c)
        for c in turn for k in range(n_dims + rep_bits - 1)
    )
    norm_state, square_state = (norm_copy, 0), (None, 0)
    squares = jnp.zeros((8, LANES), jnp.float32)
    reduced = 0
    for step, (_, k, _, c) in enumerate(events):
        if k < n_dims:
            order = stage_order(c)
            dim = order[k]
            hops[c].wait_recv()
            index = region(c, order[:k], dim, bit_of(where[dim[0]], dim[1]))
            total = work[index] + landed[k][c]
            if k + 1 < n_dims:
                work[index] = total
                start_hop(c, k + 1)
            else:
                sums[c, core, sub_rows(0), :] = total
                start_gather(c, 0)
                squares = squares + tile_sum(total * total)
                reduced += 1
                if reduced == chunks:
                    square_acc[0] = squares
                    square_state = (send(square_acc.at[0], square_got.at[0], *all_bits[0]), 0)
        else:
            for copy in gathers[c]:
                copy.wait_recv()
            start_gather(c, k - n_dims + 1)
            if reduced == chunks:
                square_state = advance_square(square_state)
        if step % 3 == 2:
            norm_state = advance_norm(norm_state)
    while norm_state[0] is not None:
        norm_state = advance_norm(norm_state)
    while square_state[0] is not None:
        square_state = advance_square(square_state)
    for c in turn:
        for copy in gathers[c]:
            copy.wait_recv()

    norm_sum = norm_acc[len(all_bits)]
    total = jnp.sum(square_acc[len(all_bits)], axis=(0, 1), keepdims=True)
    total = total + jnp.sum(norm_sum * norm_sum, axis=(0, 1), keepdims=True)
    rms = jnp.sqrt(total / entry_count)
    factor = jnp.minimum(jnp.float32(1.0), clip_rms / (rms + 1e-06))
    factor_ref[...] = jnp.broadcast_to(factor, factor_ref.shape)
    for copy in states:
        copy.wait()

    def update(refs, weights, half, base, core_index, first, count):
        rows = 32 if count % 32 == 0 else 16
        m_ref, f_ref, s_ref = refs

        def step(i, carry):
            clip = factor_ref[0:1, :]
            begin = first + i * rows
            at = pl.ds(pl.multiple_of(core_index * half + begin, rows), rows)
            for c in range(chunks):
                cols = pl.ds(c * LANES, LANES)
                grad = clip * sums[c, core_index, pl.ds(pl.multiple_of(base + begin, 8), rows), :]
                m, f, s = adamw(grad, m_ref[at, cols], f_ref[at, cols], s_ref[at, cols], 0.01)
                m_ref[at, cols] = m
                f_ref[at, cols] = f
                s_ref[at, cols] = s
                weights[at, cols] = m.astype(jnp.bfloat16)
            return carry

        lax.fori_loop(0, count // rows, step, 0)

    def update_e(core_index, first, count):
        update((state_em, state_ef, state_es), local_ew, e_half, 0, core_index, first, count)

    def update_p(core_index):
        update((state_pm, state_pf, state_ps), local_pw, p_half, e_half, core_index, 0, p_half)

    width = half_chunks * LANES
    streams = [(0, width, ascending)]
    if width < chunks * LANES:
        streams.append((width, chunks * LANES - width, ascending[::-1]))

    def e_rows(zmask, mask):
        start = flipped(shard, zmask) * (2 * e_half) + core * e_half + flipped(sub, mask) * piece
        return pl.ds(pl.multiple_of(start, 16), piece)

    def p_rows(zmask):
        start = flipped(shard, zmask) * (2 * p_half) + core * p_half
        return pl.ds(pl.multiple_of(start, 16), p_half)

    def send_e(zmask, lo, size, bit):
        cols = pl.ds(lo, size)
        if zmask == 0:
            at = pl.ds(pl.multiple_of(core * e_half + sub * piece, 16), piece)
            src = local_ew.at[at, cols]
        else:
            src = out_ew.at[e_rows(zmask, 0), cols]
        return send(src, out_ew.at[e_rows(zmask, 0), cols], "shard", bit)

    def send_p(zmask, bit):
        if zmask == 0:
            src = local_pw.at[pl.ds(pl.multiple_of(core * p_half, 16), p_half)]
        else:
            src = out_pw.at[p_rows(zmask)]
        return send(src, out_pw.at[p_rows(zmask)], "shard", bit)

    def send_n(zmask, bit):
        ref = norm_w.at[flipped(shard, zmask)]
        return send(ref, ref, "shard", bit)

    bits = list(reversed(range(shard_bits)))
    update_e(core, sub * piece, piece)
    pending = [[send_e(0, lo, size, bits[0])] for lo, size, _ in streams]
    norm_cols = norm_m.shape[1]
    mine = norm_acc[len(all_bits), :, 0:norm_cols]
    for s in range(1, shards):
        mine = jnp.where(shard == s, norm_acc[len(all_bits), :, s * norm_cols:(s + 1) * norm_cols], mine)
    m, f, s = adamw(factor_ref[0:1, 0:1] * mine, norm_m[...], norm_f[...], norm_s[...], 0.0)
    out_nm[...] = m
    out_nf[...] = f
    out_ns[...] = s
    norm_w[shard] = m
    norm_pending = [send_n(0, bits[0])]
    update_p(core)
    rest_parts = [functools.partial(update_p, other)]
    rest_parts += [
        functools.partial(update_e, core, flipped(sub, m) * piece, piece) for m in range(1, subs)
    ]
    rest_parts.append(functools.partial(update_e, other, 0, e_half))
    rest_parts.reverse()
    rest_parts.pop(0)()
    held = [0, 1 << bits[0]]
    proj_pending = []
    for n, b in enumerate(bits[1:]):
        for i, (lo, size, _) in enumerate(streams):
            for copy in pending[i]:
                copy.wait_recv()
            pending[i] = [send_e(z, lo, size, b) for z in held]
        for copy in norm_pending:
            copy.wait_recv()
        norm_pending = [send_n(z, b) for z in held]
        if n == 0:
            proj_pending = [send_p(0, bits[0])]
        held = held + [z | 1 << b for z in held]
    if not proj_pending:
        proj_pending = [send_p(0, bits[0])]
    for part in rest_parts:
        part()
    outs = [
        local(src, dst)
        for src, dst in (
            (local_ew, out_ew.at[pl.ds(pl.multiple_of(shard * (2 * e_half), 16), 2 * e_half)]),
            (local_pw, out_pw.at[pl.ds(pl.multiple_of(shard * (2 * p_half), 16), 2 * p_half)]),
            (state_em, out_em), (state_ef, out_ef), (state_es, out_es),
            (state_pm, out_pm), (state_pf, out_pf), (state_ps, out_ps),
        )
    ]
    proj_held = [0, 1 << bits[0]]
    proj_bits = bits[1:]

    def advance_proj():
        nonlocal proj_pending, proj_held, proj_bits
        if proj_bits:
            b, proj_bits = proj_bits[0], proj_bits[1:]
            for copy in proj_pending:
                copy.wait_recv()
            proj_pending = [send_p(z, b) for z in proj_held]
            proj_held = proj_held + [z | 1 << b for z in proj_held]

    masks = [[0] for _ in streams]
    fresh = [[0] for _ in streams]
    last = []

    def send_core(i):
        lo, size, _ = streams[i]
        for m in fresh[i]:
            for z in range(1, shards):
                ref = out_ew.at[e_rows(z, m), pl.ds(lo, size)]
                last.append(send(ref, ref, "rep", 0))

    for t in range(rep_bits - 1):
        for i, (lo, size, order) in enumerate(streams):
            for copy in pending[i]:
                copy.wait_recv()
            pending[i] = []
            for m in masks[i]:
                for z in range(1, shards):
                    ref = out_ew.at[e_rows(z, m), pl.ds(lo, size)]
                    pending[i].append(send(ref, ref, "rep", order[t]))
            send_core(i)
            fresh[i] = [m | 1 << (order[t] - 1) for m in masks[i]]
            masks[i] = masks[i] + fresh[i]
        advance_proj()
    while proj_bits:
        advance_proj()
    for copy in proj_pending + norm_pending:
        copy.wait_recv()
    for z in range(1, shards):
        ref = out_pw.at[p_rows(z)]
        last.append(send(ref, ref, "rep", 0))
    for i, (lo, size, _) in enumerate(streams):
        for copy in pending[i]:
            copy.wait_recv()
        send_core(i)
    out_nw[...] = norm_w[...]
    for copy in last:
        copy.wait_recv()
    for copy in sends:
        copy.wait_send()
    for copy in outs:
        copy.wait()


def shards_fn(
    reps,
    shards,
    grad_embed, grad_proj, grad_norms,
    embed_master, embed_first, embed_second,
    proj_master, proj_first, proj_second,
    norm_master, norm_first, norm_second,
):
    embed_rows, width = grad_embed.shape[2:]
    proj_rows = grad_proj.shape[2]
    norm_rows, norm_cols = norm_master.shape
    chunks = width // LANES
    e_half = embed_rows // shards // 2
    p_half = proj_rows // shards // 2
    subs = reps // 2
    unit = 8 * subs
    half_rows = -(-(e_half + p_half) // unit) * unit
    block = half_rows // subs
    entry_count = float((embed_rows + proj_rows + norm_rows) * width)
    rep_bits = reps.bit_length() - 1
    shard_bits = shards.bit_length() - 1
    all_bits = rep_bits + shard_bits
    n_dims = all_bits - 1
    f32, bf16 = jnp.float32, jnp.bfloat16
    n_streams = 2 if chunks > 1 else 1
    copies = 2 * chunks + 2 * all_bits + chunks * n_dims + chunks * subs
    copies += (n_streams + 2) * (shards - 1) + n_streams * (shards - 1) * subs
    copies += n_streams * (shards - 1) * subs + (shards - 1)
    plan = (reps, shards, chunks, e_half, p_half, half_rows, entry_count)
    any_spec = pl.BlockSpec(memory_space=pl.ANY)
    vmem_spec = pl.BlockSpec(memory_space=pltpu.VMEM)
    e_part, p_part = (2 * e_half, width), (2 * p_half, width)
    landed = [
        pltpu.VMEM((chunks,) + (2,) * (n_dims - 1 - k) + (block, LANES), f32) for k in range(n_dims)
    ]
    outs = pl.pallas_call(
        functools.partial(kernel, plan),
        out_shape=(
            [jax.ShapeDtypeStruct(e_part, f32)] * 3
            + [jax.ShapeDtypeStruct((embed_rows, width), bf16)]
            + [jax.ShapeDtypeStruct(p_part, f32)] * 3
            + [jax.ShapeDtypeStruct((proj_rows, width), bf16)]
            + [jax.ShapeDtypeStruct((norm_rows, norm_cols), f32)] * 3
            + [jax.ShapeDtypeStruct((shards, norm_rows, norm_cols), f32)]
        ),
        in_specs=[any_spec] * 2 + [vmem_spec] + [any_spec] * 6 + [vmem_spec] * 3,
        out_specs=[any_spec] * 8 + [vmem_spec] * 4,
        scratch_shapes=[
            pltpu.VMEM((chunks, shards, e_half, LANES), bf16),
            pltpu.VMEM((chunks, shards, p_half, LANES), bf16),
            pltpu.VMEM((chunks, shards, e_half, LANES), bf16),
            pltpu.VMEM((chunks, shards, p_half, LANES), bf16),
            pltpu.VMEM((chunks,) + (2,) * n_dims + (block, LANES), f32),
            pltpu.VMEM((chunks, 2, half_rows, LANES), f32),
            pltpu.VMEM(e_part, f32), pltpu.VMEM(e_part, f32), pltpu.VMEM(e_part, f32),
            pltpu.VMEM(p_part, f32), pltpu.VMEM(p_part, f32), pltpu.VMEM(p_part, f32),
            pltpu.VMEM(e_part, bf16), pltpu.VMEM(p_part, bf16),
            pltpu.VMEM((all_bits + 1, norm_rows, width), f32),
            pltpu.VMEM((all_bits, norm_rows, width), f32),
            pltpu.VMEM((shards, norm_rows, norm_cols), f32),
            pltpu.VMEM((all_bits + 1, 8, LANES), f32),
            pltpu.VMEM((all_bits, 8, LANES), f32),
            pltpu.VMEM((8, LANES), f32),
        ]
        + landed
        + [
            pltpu.SemaphoreType.DMA((copies,)),
            pltpu.SemaphoreType.DMA((copies,)),
            pltpu.SemaphoreType.DMA((2 * chunks + 14,)),
        ],
        compiler_params=pltpu.CompilerParams(
            collective_id=0, has_side_effects=True, vmem_limit_bytes=58 * 1024 * 1024
        ),
    )(
        grad_embed.reshape(shards, 2, e_half, width),
        grad_proj.reshape(shards, 2, p_half, width),
        grad_norms[0, 0],
        embed_master, embed_first, embed_second,
        proj_master, proj_first, proj_second,
        norm_master, norm_first, norm_second,
    )
    norm_weights = outs[11].astype(bf16).transpose(1, 0, 2).reshape(norm_rows, width)
    return tuple(outs[:11]) + (norm_weights,)


def solution(mesh):
    grad, part, whole = P("rep", "shard", None, None), P("shard", None), P()
    cols = P(None, "shard")
    return jax.shard_map(
        functools.partial(shards_fn, mesh.shape["rep"], mesh.shape["shard"]),
        mesh=mesh,
        in_specs=(grad,) * 3 + (part,) * 6 + (cols,) * 3,
        out_specs=(part,) * 3 + (whole,) + (part,) * 3 + (whole,) + (cols,) * 3 + (whole,),
        check_vma=False,
    )
```
